256 devices in a mesh: group: 2 (over y_hi), dp: 16 (over z, core), tensor: 8 (over y_lo, x).
Axes of the slice: x: 4, y: 4 (y_hi: 2, y_lo: 2; y = y_hi * 2 + y_lo), z: 8, core: 2. Of those that a mesh axis runs over, the one named last changes fastest.
Arguments:
- features: bfloat16 [65536, 8192], P(('group', 'dp'), 'tensor'), may hold values from -6 to 6
- cotangent: bfloat16 [65536, 2048], P(('group', 'dp'), 'tensor'), may hold values from -6 to 6
- master: float32 [8192, 2048], P(('group', 'dp'), 'tensor'), may hold values from -6 to 6
- first_moment: float32 [8192, 2048], P(('group', 'dp'), 'tensor'), may hold values from -1.8 to 1.8
- second_moment: float32 [8192, 2048], P(('group', 'dp'), 'tensor'), may hold values from 0.01 to 1
- queries: bfloat16 [64, 8192], P(('group', 'dp'), 'tensor')
- key_cache: bfloat16 [64, 2048, 1024], P(('group', 'dp'), None, 'tensor'), may hold values from -4 to 4
- value_cache: bfloat16 [64, 2048, 1024], P(('group', 'dp'), None, 'tensor'), may hold values from -6 to 6
- new_kv: bfloat16 [64, 2048], P(('group', 'dp'), 'tensor'), may hold values from -6 to 6
- lengths: int32 [64], P(('group', 'dp')), may hold values from 2 to 2048, as said below
Outputs:
- master_out: float32 [8192, 2048], P(('group', 'dp'), 'tensor')
- first_out: float32 [8192, 2048], P(('group', 'dp'), 'tensor')
- second_out: float32 [8192, 2048], P(('group', 'dp'), 'tensor')
- rollout_weights: bfloat16 [8192, 2048], P(None, 'tensor')
- attended: bfloat16 [64, 8192], P(('group', 'dp'), 'tensor')
The draws below stay inside these ranges and needn't reach their ends.
Inputs may be any that keep to these rules, and one draw needn't show every extreme that they name: `lengths`: some decode row uses all 2048 positions.
All inputs are finite; a program needn't handle non-finite values.
Results may differ from the reference program's by a relative error of at most 0.01.
Values may be sent and summed in bfloat16 or wider, within the bound.
No kernel may reach another device: no remote copies, remote signals or barrier semaphores. Data moves between devices by JAX's collectives and lax.ppermute only.
A program may use at most 128 MiB of HBM per device.

```python
import math
import jax
import jax.numpy as jnp
from jax import lax

D = 8192
QH = 64
KVH = 8
HD = 128
KVC = 2048
TOKENS = 65536
ROWS = 64
CACHE = 2048


def cache_keys(key):
    base = jax.random.normal(jax.random.fold_in(key, 101), (ROWS, CACHE, KVH * HD), jnp.float32)
    return jnp.clip(base, -4.0, 4.0)


def draw_key_cache(key, part):
    base = cache_keys(key)
    return base.astype(jnp.bfloat16)


def draw_queries(key, part):
    key = jax.random.fold_in(key, 7)
    entries = jnp.clip(jax.random.normal(key, (ROWS, QH * HD), jnp.float32), -4.0, 4.0)
    return entries.astype(jnp.bfloat16)


def draw_lengths(key, part):
    key = jax.random.fold_in(key, 3)
    drawn = jax.random.randint(jax.random.fold_in(key, 1), (ROWS,), 2, CACHE + 1, dtype=jnp.int32)
    chosen = jax.random.randint(jax.random.fold_in(key, 2), (), 0, ROWS, dtype=jnp.int32)
    return jnp.where(jnp.arange(ROWS, dtype=jnp.int32) == chosen, CACHE, drawn).astype(jnp.int32)


def spiked(values, rng, source, target, shards_of, factor):
    owner, partner = [(jnp.arange(values.shape[axis_at]) // (values.shape[axis_at] // shards_of)).reshape([-1 if axis == axis_at else 1 for axis in range(values.ndim)]) for axis_at in (source, target)]
    chosen = jax.random.permutation(rng, shards_of)[partner]
    strong = (owner == chosen) | (owner == (partner + shards_of // 2) % shards_of)
    return jnp.where(strong, factor * values, values)


def block_levels(rng, extent, shards, smallest, largest):
    def one(position, blocks):
        steps = jax.random.uniform(jax.random.fold_in(jax.random.fold_in(rng, 6), position), (blocks,), jnp.float32, smallest / len(shards), largest / len(shards))
        return jnp.repeat(jnp.exp(steps), extent[position] // blocks).reshape((-1,) + (1,) * (len(extent) - position - 1))

    level = one(*shards[0])
    for cut in shards[1:]:
        level = level * one(*cut)
    return level


def gaussian(stream_key, dims, scale, limit, pieces=(), kind=jnp.bfloat16):
    factor_of = block_levels(stream_key, dims, pieces, -0.22, 0.18) if pieces else 1.0
    values = jax.random.normal(stream_key, dims, jnp.float32) * scale * factor_of
    return jnp.minimum(jnp.maximum(values, -limit), limit).astype(kind)


def noise_with(stream_key, extent, scale, bound, pieces, heavy, held_as=jnp.bfloat16):
    array = scale * jax.random.normal(stream_key, extent, jnp.float32)
    if pieces:
        array = array * block_levels(stream_key, extent, pieces, -0.22, 0.18)
    return jnp.clip(spiked(array, jax.random.fold_in(stream_key, 3), *heavy), -bound, bound).astype(held_as)


def setup_inputs(seed: int = 0) -> dict:
    arg_keys = jax.random.split(jax.random.key(seed), 11)
    return {
        "features": noise_with(arg_keys[0], (TOKENS, D), 1.0, 6.0, ((0, 32), (1, 8)), (0, 1, 32, 2.75)),
        "cotangent": gaussian(arg_keys[1], (TOKENS, KVC), 1.0, 6.0, ((0, 32), (1, 8))),
        "master": gaussian(arg_keys[2], (D, KVC), 1.0, 6.0, ((0, 32), (1, 8)), jnp.float32),
        "first_moment": gaussian(arg_keys[3], (D, KVC), 0.3, 1.8, ((0, 32), (1, 8)), jnp.float32),
        "second_moment": jnp.clip(jnp.exp(math.log(1.0) - 4.6051702 * jax.random.uniform(arg_keys[4], (D, KVC), jnp.float32) ** block_levels(arg_keys[4], (D, KVC), ((0, 32), (1, 8)), -0.2, 0.2)), 0.01, 1.0),
        "queries": draw_queries(jax.random.fold_in(arg_keys[10], 71), 0),
        "key_cache": draw_key_cache(jax.random.fold_in(arg_keys[10], 71), 0),
        "value_cache": gaussian(arg_keys[7], (ROWS, CACHE, KVH * HD), 1.0, 6.0, ((0, 32), (2, 8))),
        "new_kv": gaussian(arg_keys[8], (ROWS, KVC), 1.0, 6.0, ((0, 32), (1, 8))),
        "lengths": draw_lengths(jax.random.fold_in(arg_keys[10], 71), 0),
    }


beta_one = 0.9
beta_two = 0.95
adam_eps = 1e-08
learn_rate = 0.05
decay_rate = 0.1
bias_first = 1.0 - 0.9 ** 10
bias_second = 1.0 - 0.95 ** 10

def decode_row(items):
    query_row, key_rows, value_rows, fresh_row, length_row = items
    groups = QH // KVH
    query_f = query_row.reshape(KVH, groups, HD).astype(jnp.float32)
    key_f = key_rows.reshape(CACHE, KVH, HD).astype(jnp.float32)
    value_f = value_rows.reshape(CACHE, KVH, HD).astype(jnp.float32)
    fresh = fresh_row.reshape(KVH, 2, HD).astype(jnp.float32)
    scale = HD ** (-0.5)
    scores = jnp.einsum('kgd,lkd->kgl', query_f, key_f) * scale
    visible = jnp.arange(CACHE, dtype=jnp.int32) < length_row
    scores = jnp.where(visible[None, None, :], scores, -jnp.inf)
    own_score = jnp.einsum('kgd,kd->kg', query_f, fresh[:, 0, :]) * scale
    top = jnp.maximum(lax.optimization_barrier(jnp.max(scores, axis=-1)), own_score)
    expo = jnp.exp(scores - top[..., None])
    own_expo = jnp.exp(own_score - top)
    total = lax.optimization_barrier(jnp.sum(expo, axis=-1)) + own_expo
    weights = (expo / total[..., None]).astype(jnp.bfloat16)
    own_weight = (own_expo / total).astype(jnp.bfloat16)
    mixed = jnp.einsum('kgl,lkd->kgd', weights.astype(jnp.float32), value_f)
    mixed = mixed + own_weight.astype(jnp.float32)[..., None] * fresh[:, 1, None, :]
    return mixed.reshape(QH * HD).astype(jnp.bfloat16)

def reference(features, cotangent, master, first_moment, second_moment, queries, key_cache, value_cache, new_kv, lengths):
    gradient = jnp.dot(features.T, cotangent, preferred_element_type=jnp.float32) * TOKENS ** (-0.5)
    first_out = beta_one * first_moment + (1.0 - beta_one) * gradient
    second_out = beta_two * second_moment + (1.0 - beta_two) * gradient * gradient
    step_dir = first_out / bias_first / (jnp.sqrt(second_out / bias_second) + adam_eps) + decay_rate * master
    master_out = master - learn_rate * step_dir
    rollout_weights = master_out.astype(jnp.bfloat16)
    attended = lax.map(decode_row, (queries, key_cache, value_cache, new_kv, lengths))
    return (master_out, first_out, second_out, rollout_weights, attended)
```

```python
import functools

import jax
import jax.numpy as jnp
from jax import lax
from jax.experimental import pallas as pl
from jax.experimental.pallas import tpu as pltpu
from jax.sharding import Mesh
from jax.sharding import PartitionSpec as P

QH = 64
KVH = 8
HD = 128
GROUPS = QH // KVH
BLK = 256

beta_one = 0.9
beta_two = 0.95
adam_eps = 1e-08
learn_rate = 0.05
decay_rate = 0.1
bias_first = 1.0 - 0.9**10
bias_second = 1.0 - 0.95**10

AXES = ("group", "z", "core", "ylo", "x")
SIZES = (2, 8, 2, 2, 4)
VMEM_SPEC = pl.BlockSpec(memory_space=pltpu.VMEM)
SMEM_SPEC = pl.BlockSpec(memory_space=pltpu.SMEM)
ANY_SPEC = pl.BlockSpec(memory_space=pl.ANY)
PARAMS = pltpu.CompilerParams(vmem_limit_bytes=32 * 1024 * 1024)
BF = jnp.bfloat16
F32 = jnp.float32


def shift(value, axis, by):
    size = SIZES[AXES.index(axis)]
    return lax.ppermute(value, axis, [(i, (i + by) % size) for i in range(size)])


def flat(g, z, core, ylo, x):
    return (((g * 8 + z) * 2 + core) * 2 + ylo) * 4 + x


def attend_kernel(lengths_ref, q_ref, k_ref, v_ref, fresh_ref, out_ref):
    scale = HD ** (-0.5)
    rows, span, _ = k_ref.shape
    for r in range(rows):
        q = q_ref[r]
        scores = (
            lax.dot_general(q, k_ref[r], (((1,), (1,)), ((), ())), preferred_element_type=F32)
            * scale
        )
        at = lax.broadcasted_iota(jnp.int32, (GROUPS, span), 1)
        scores = jnp.where(at < lengths_ref[r], scores, -jnp.inf)
        fresh = fresh_ref[r : r + 1, :]
        new_k = fresh[:, :HD].astype(F32)
        new_v = fresh[:, HD:].astype(F32)
        own = jnp.sum(q.astype(F32) * new_k, axis=-1, keepdims=True) * scale
        top = jnp.maximum(jnp.max(scores, axis=-1, keepdims=True), own)
        expo = jnp.exp(scores - top)
        own_expo = jnp.exp(own - top)
        total = jnp.sum(expo, axis=-1, keepdims=True) + own_expo
        weights = (expo / total).astype(BF)
        own_weight = (own_expo / total).astype(BF).astype(F32)
        mixed = jnp.dot(weights, v_ref[r], preferred_element_type=F32)
        out_ref[r] = (mixed + own_weight * new_v).astype(BF)


def attend(queries, key_cache, value_cache, new_kv, lengths):
    rows = queries.shape[0]
    span = key_cache.shape[1]
    out = pl.pallas_call(
        attend_kernel,
        out_shape=jax.ShapeDtypeStruct((rows, GROUPS, HD), BF),
        in_specs=[SMEM_SPEC] + [VMEM_SPEC] * 4,
        out_specs=VMEM_SPEC,
        compiler_params=PARAMS,
        cost_estimate=pl.CostEstimate(
            flops=4 * rows * GROUPS * span * HD,
            bytes_accessed=4 * rows * span * HD,
            transcendentals=rows * GROUPS * span,
        ),
        name="attend",
    )(lengths, queries.reshape(rows, GROUPS, HD), key_cache, value_cache, new_kv)
    return out.reshape(rows, GROUPS * HD)


def product_kernel(pieces, where_ref, f_ref, *refs):
    keep_ref, send_ref = refs[-2:]
    core = where_ref[0]
    z = where_ref[1]
    at = 0
    for m, rows in enumerate(pieces):
        chunk = refs[at : at + len(rows)]
        at += len(rows)
        for high in range(2):
            slot = lax.rem(2 * m + high - z + 8, 8)
            for sent, out_ref in ((0, keep_ref), (1, send_ref)):
                parity = core if sent == 0 else 1 - core
                cols = pl.ds(pl.multiple_of((2 * high + parity) * BLK, BLK), BLK)
                total = jnp.zeros((BLK, BLK), F32)
                start = 0
                for c_ref, count in zip(chunk, rows):
                    total += lax.dot_general(
                        c_ref[...],
                        f_ref[start : start + count, cols],
                        (((0,), (0,)), ((), ())),
                        preferred_element_type=F32,
                    )
                    start += count
                out_ref[slot] = total.astype(BF)


def product(where, features, chunks):
    pieces = tuple(tuple(c.shape[0] for c in chunk) for chunk in chunks)
    flat_chunks = [c for chunk in chunks for c in chunk]
    shape = jax.ShapeDtypeStruct((8, BLK, BLK), BF)
    return pl.pallas_call(
        functools.partial(product_kernel, pieces),
        out_shape=(shape, shape),
        in_specs=[SMEM_SPEC] + [VMEM_SPEC] * (1 + len(flat_chunks)),
        out_specs=(VMEM_SPEC, VMEM_SPEC),
        compiler_params=PARAMS,
        cost_estimate=pl.CostEstimate(
            flops=2 * 2048 * 1024 * 1024, bytes_accessed=10 * 1024 * 1024, transcendentals=0
        ),
        name="product",
    )(where, features, *flat_chunks)


def pair_kernel(keep_ref, got_ref, a3_ref, a5_ref, lo_ref, hi_ref, a1_ref, a7_ref, rest_ref):
    def both(slot):
        return (keep_ref[slot].astype(F32) + got_ref[slot].astype(F32)).astype(BF)

    a3_ref[...] = both(3)
    a5_ref[...] = both(5)
    middle = both(4)
    half = BLK // 2
    lo_ref[...] = middle[:half]
    hi_ref[...] = middle[half:]
    a1_ref[...] = both(1)
    a7_ref[...] = both(7)
    for at, slot in enumerate((0, 2, 6)):
        rest_ref[at] = both(slot)


def second_kernel(rest_ref, r3_ref, r5_ref, lo_ref, hi_ref, b2_ref, b6_ref):
    half = BLK // 2
    b2 = rest_ref[1].astype(F32) + r3_ref[...].astype(F32)
    b6 = rest_ref[2].astype(F32) + r5_ref[...].astype(F32)
    b2_ref[:half] = (b2[:half] + lo_ref[...].astype(F32)).astype(BF)
    b2_ref[half:] = b2[half:].astype(BF)
    b6_ref[:half] = b6[:half].astype(BF)
    b6_ref[half:] = (b6[half:] + hi_ref[...].astype(F32)).astype(BF)


def third_kernel(rest_ref, m1_ref, p1_ref, m2_ref, p2_ref, out_ref):
    total = rest_ref[0].astype(F32)
    for ref in (m1_ref, p1_ref, m2_ref, p2_ref):
        total += ref[...].astype(F32)
    out_ref[...] = total.astype(BF)


def small_call(body, out_shape, *args, name):
    many = isinstance(out_shape, tuple)
    return pl.pallas_call(
        body,
        out_shape=out_shape,
        in_specs=[VMEM_SPEC] * len(args),
        out_specs=tuple([VMEM_SPEC] * len(out_shape)) if many else VMEM_SPEC,
        compiler_params=PARAMS,
        cost_estimate=pl.CostEstimate(
            flops=1 << 20, bytes_accessed=2 * 1024 * 1024, transcendentals=0
        ),
        name=name,
    )(*args)


def reduce_macro(keep, send):
    block = jax.ShapeDtypeStruct((BLK, BLK), BF)
    half = jax.ShapeDtypeStruct((BLK // 2, BLK), BF)
    got = shift(send, "core", 1)
    a3, a5, lo, hi, a1, a7, rest = small_call(
        pair_kernel,
        (block, block, half, half, block, block, jax.ShapeDtypeStruct((3, BLK, BLK), BF)),
        keep,
        got,
        name="pair",
    )
    r3 = shift(a3, "z", 1)
    r5 = shift(a5, "z", -1)
    r_lo = shift(lo, "z", 2)
    r_hi = shift(hi, "z", -2)
    b2, b6 = small_call(second_kernel, (block, block), rest, r3, r5, r_lo, r_hi, name="second")
    m1 = shift(a1, "z", 1)
    p1 = shift(a7, "z", -1)
    m2 = shift(b2, "z", 2)
    p2 = shift(b6, "z", -2)
    return small_call(third_kernel, block, rest, m1, p1, m2, p2, name="third")


def to_owner(block, chunk_of):
    got = []
    for g in range(2):
        pairs = []
        for z in range(8):
            for core in range(2):
                for ylo in range(2):
                    for x in range(4):
                        to_ylo, to_x = chunk_of(z // 2, ylo, x)
                        pairs.append(
                            (flat(g, z, core, ylo, x), flat(ylo, 2 * x + z % 2, core, to_ylo, to_x))
                        )
        got.append(lax.ppermute(block, AXES, pairs))
    return got


def update_kernel(scale, a_ref, b_ref, c_ref, d_ref, w_ref, m_ref, v_ref, wo, mo, vo, ro):
    total = a_ref[...].astype(F32) + b_ref[...].astype(F32)
    total += c_ref[...].astype(F32) + d_ref[...].astype(F32)
    gradient = total.T * scale
    first = beta_one * m_ref[...] + (1.0 - beta_one) * gradient
    second = beta_two * v_ref[...] + (1.0 - beta_two) * gradient * gradient
    master = w_ref[...]
    step = first / bias_first / (jnp.sqrt(second / bias_second) + adam_eps) + decay_rate * master
    master = master - learn_rate * step
    wo[...] = master
    mo[...] = first
    vo[...] = second
    ro[...] = master.astype(BF)


def place_kernel(layout, where_ref, *refs):
    out_ref, sem = refs[-2:]
    group, z, core = where_ref[2], where_ref[1], where_ref[0]
    copies = []
    for ref, blocks in zip(refs, layout):
        at = 0
        for flip_g, dz, flip_c, first, rows in blocks:
            g = 1 - group if flip_g else group
            c = 1 - core if flip_c else core
            zz = lax.rem(z + dz + 8, 8)
            row = pl.multiple_of((g * 16 + zz * 2 + c) * BLK + first, BLK // 2)
            copies.append(
                pltpu.make_async_copy(
                    ref.at[pl.ds(at, rows), :], out_ref.at[pl.ds(row, rows), :], sem.at[len(copies)]
                )
            )
            at += rows
    for copy in copies:
        copy.start()
    for copy in copies:
        copy.wait()


def gather_rows(where, own):
    half = BLK // 2

    def blocks(flip_g, flip_c, which):
        names = {
            "own": (0, 0, BLK),
            "m1": (-1, 0, BLK),
            "p1": (1, 0, BLK),
            "m2": (-2, 0, BLK),
            "p2": (2, 0, BLK),
            "m3": (-3, 0, BLK),
            "p3": (3, 0, BLK),
            "lo": (4, 0, half),
            "hi": (4, half, half),
        }
        return [(flip_g, names[n][0], flip_c, names[n][1], names[n][2]) for n in which]

    m1 = shift(own, "z", 1)
    p1 = shift(own, "z", -1)
    m2 = shift(own, "z", 2)
    p2 = shift(own, "z", -2)
    other = shift(own, "group", 1)
    near = ["m1", "p1", "m2", "p2"]
    far = ["m3", "p3", "lo", "hi"]
    first = jnp.concatenate([m1, p1, m2, p2])
    m3 = shift(m2, "z", 1)
    p3 = shift(p2, "z", -1)
    lo = shift(m2[:half], "z", 2)
    hi = shift(p2[half:], "z", -2)
    other_near = shift(first, "group", 1)
    core_one = shift(jnp.concatenate([own, first, other]), "core", 1)
    second = jnp.concatenate([m3, p3, lo, hi])
    other_far = shift(second, "group", 1)
    core_two = shift(jnp.concatenate([second, other_near]), "core", 1)
    core_three = shift(other_far, "core", 1)
    sources = [
        (own, blocks(0, 0, ["own"])),
        (first, blocks(0, 0, near)),
        (second, blocks(0, 0, far)),
        (other, blocks(1, 0, ["own"])),
        (other_near, blocks(1, 0, near)),
        (other_far, blocks(1, 0, far)),
        (core_one, blocks(0, 1, ["own"] + near) + blocks(1, 1, ["own"])),
        (core_two, blocks(0, 1, far) + blocks(1, 1, near)),
        (core_three, blocks(1, 1, far)),
    ]
    return pl.pallas_call(
        functools.partial(place_kernel, tuple(tuple(b) for _, b in sources)),
        out_shape=jax.ShapeDtypeStruct((32 * BLK, BLK), BF),
        in_specs=[SMEM_SPEC] + [ANY_SPEC] * len(sources),
        out_specs=ANY_SPEC,
        scratch_shapes=[pltpu.SemaphoreType.DMA((sum(len(b) for _, b in sources),))],
        compiler_params=PARAMS,
        cost_estimate=pl.CostEstimate(flops=0, bytes_accessed=8 * 1024 * 1024, transcendentals=0),
        name="place",
    )(where, *[s for s, _ in sources])


def local(
    features,
    cotangent,
    master,
    first_moment,
    second_moment,
    queries,
    key_cache,
    value_cache,
    new_kv,
    lengths,
):
    tokens = features.shape[0]
    scale = float(tokens * 32) ** (-0.5)
    where = jnp.stack(
        [lax.axis_index("core"), lax.axis_index("z"), lax.axis_index("group")]
    ).astype(jnp.int32)
    half = tokens // 2

    xm = shift(cotangent, "x", 1)
    xp = shift(cotangent, "x", -1)
    mate = shift(cotangent, "ylo", 1)
    far_lo = shift(xm[:half], "x", 1)
    far_hi = shift(xp[half:], "x", -1)
    bm_lo = shift(mate[:half], "x", 1)
    bp_hi = shift(mate[half:], "x", -1)
    bm_hi = shift(xm[half:], "ylo", 1)
    bp_lo = shift(xp[:half], "ylo", 1)
    c1, c2 = 768, 1280
    bf_lo = shift(bm_lo[:c1], "x", 1)
    bf_hi = shift(bp_hi[c2 - half :], "x", -1)
    bf_mid = shift(jnp.concatenate([far_lo[c1:], far_hi[: c2 - half]]), "ylo", 1)

    attended = attend(queries, key_cache, value_cache, new_kv, lengths)

    keep_a, send_a = product(where, features, [[cotangent], [xm], [xp], [mate]])
    block_a = reduce_macro(keep_a, send_a)

    def chunk_a(m, ylo, x):
        return [(ylo, x), (ylo, (x - 1) % 4), (ylo, (x + 1) % 4), (1 - ylo, x)][m]

    got_a = to_owner(block_a, chunk_a)

    keep_b, send_b = product(
        where, features, [[far_lo, far_hi], [bm_lo, bm_hi], [bp_lo, bp_hi], [bf_lo, bf_mid, bf_hi]]
    )
    block_b = reduce_macro(keep_b, send_b)

    def chunk_b(m, ylo, x):
        return [(ylo, (x + 2) % 4), (1 - ylo, (x - 1) % 4), (1 - ylo, (x + 1) % 4), (1 - ylo, (x + 2) % 4)][m]

    got_b = to_owner(block_b, chunk_b)

    out32 = jax.ShapeDtypeStruct((BLK, BLK), F32)
    master_out, first_out, second_out, own = small_call(
        functools.partial(update_kernel, scale),
        (out32, out32, out32, jax.ShapeDtypeStruct((BLK, BLK), BF)),
        *got_a,
        *got_b,
        master,
        first_moment,
        second_moment,
        name="update",
    )
    rollout = gather_rows(where, own)
    return (master_out, first_out, second_out, rollout, attended)


def solution(mesh):
    fine = Mesh(mesh.devices.reshape(SIZES), AXES)
    rows, cols = ("group", "z", "core"), ("ylo", "x")
    return jax.shard_map(
        local,
        mesh=fine,
        in_specs=(
            P(rows, cols),
            P(rows, cols),
            P(rows, cols),
            P(rows, cols),
            P(rows, cols),
            P(rows, cols),
            P(rows, None, cols),
            P(rows, None, cols),
            P(rows, cols),
            P(rows),
        ),
        out_specs=(
            P(rows, cols),
            P(rows, cols),
            P(rows, cols),
            P(None, cols),
            P(rows, cols),
        ),
        check_vma=False,
    )
```

```python
import functools

import jax
import jax.numpy as jnp
from jax import lax
from jax.experimental import pallas as pl
from jax.experimental.pallas import tpu as pltpu
from jax.sharding import Mesh
from jax.sharding import PartitionSpec as P

QH = 64
KVH = 8
HD = 128
GROUPS = QH // KVH
BLK = 256

beta_one = 0.9
beta_two = 0.95
adam_eps = 1e-08
learn_rate = 0.05
decay_rate = 0.1
bias_first = 1.0 - 0.9**10
bias_second = 1.0 - 0.95**10

AXES = ("group", "z", "core", "ylo", "x")
SIZES = (2, 8, 2, 2, 4)
VMEM_SPEC = pl.BlockSpec(memory_space=pltpu.VMEM)
SMEM_SPEC = pl.BlockSpec(memory_space=pltpu.SMEM)
ANY_SPEC = pl.BlockSpec(memory_space=pl.ANY)
PARAMS = pltpu.CompilerParams(vmem_limit_bytes=32 * 1024 * 1024)
BF = jnp.bfloat16
F32 = jnp.float32


def shift(value, axis, by):
    size = SIZES[AXES.index(axis)]
    return lax.ppermute(value, axis, [(i, (i + by) % size) for i in range(size)])


def after(value, *marks):
    return lax.optimization_barrier((value, *marks))[0]


def flat(g, z, core, ylo, x):
    return (((g * 8 + z) * 2 + core) * 2 + ylo) * 4 + x


def attend_kernel(lengths_ref, q_ref, k_ref, v_ref, fresh_ref, out_ref):
    scale = HD ** (-0.5)
    rows, span, _ = k_ref.shape
    for r in range(rows):
        q = q_ref[r]
        scores = (
            lax.dot_general(q, k_ref[r], (((1,), (1,)), ((), ())), preferred_element_type=F32)
            * scale
        )
        at = lax.broadcasted_iota(jnp.int32, (GROUPS, span), 1)
        scores = jnp.where(at < lengths_ref[r], scores, -jnp.inf)
        fresh = fresh_ref[r : r + 1, :]
        new_k = fresh[:, :HD].astype(F32)
        new_v = fresh[:, HD:].astype(F32)
        own = jnp.sum(q.astype(F32) * new_k, axis=-1, keepdims=True) * scale
        top = jnp.maximum(jnp.max(scores, axis=-1, keepdims=True), own)
        expo = jnp.exp(scores - top)
        own_expo = jnp.exp(own - top)
        total = jnp.sum(expo, axis=-1, keepdims=True) + own_expo
        weights = (expo / total).astype(BF)
        own_weight = (own_expo / total).astype(BF).astype(F32)
        mixed = jnp.dot(weights, v_ref[r], preferred_element_type=F32)
        out_ref[r] = (mixed + own_weight * new_v).astype(BF)


def attend(queries, key_cache, value_cache, new_kv, lengths):
    rows = queries.shape[0]
    span = key_cache.shape[1]
    out = pl.pallas_call(
        attend_kernel,
        out_shape=jax.ShapeDtypeStruct((rows, GROUPS, HD), BF),
        in_specs=[SMEM_SPEC] + [VMEM_SPEC] * 4,
        out_specs=VMEM_SPEC,
        compiler_params=PARAMS,
        cost_estimate=pl.CostEstimate(
            flops=4 * rows * GROUPS * span * HD,
            bytes_accessed=4 * rows * span * HD,
            transcendentals=rows * GROUPS * span,
        ),
        name="attend",
    )(lengths, queries.reshape(rows, GROUPS, HD), key_cache, value_cache, new_kv)
    return out.reshape(rows, GROUPS * HD)


def product_kernel(chunks, where_ref, f_ref, *refs):
    keep_ref, send_ref = refs[-2:]
    core = where_ref[0]
    for m, pieces in enumerate(chunks):
        for high in range(2):
            for parity, out_ref in ((core, keep_ref), (1 - core, send_ref)):
                cols = pl.ds(pl.multiple_of((2 * high + parity) * BLK, BLK), BLK)
                total = jnp.zeros((BLK, BLK), F32)
                row = 0
                for i, start, count in pieces:
                    total += lax.dot_general(
                        refs[i][start : start + count],
                        f_ref[row : row + count, cols],
                        (((0,), (0,)), ((), ())),
                        preferred_element_type=F32,
                    )
                    row += count
                out_ref[2 * m + high] = total.astype(BF)


def product(where, features, arrays, chunks, name):
    shape = jax.ShapeDtypeStruct((2 * len(chunks), BLK, BLK), BF)
    return pl.pallas_call(
        functools.partial(product_kernel, chunks),
        out_shape=(shape, shape),
        in_specs=[SMEM_SPEC] + [VMEM_SPEC] * (1 + len(arrays)),
        out_specs=(VMEM_SPEC, VMEM_SPEC),
        compiler_params=PARAMS,
        cost_estimate=pl.CostEstimate(
            flops=2 * 2048 * 1024 * 256 * len(chunks),
            bytes_accessed=10 * 1024 * 1024,
            transcendentals=0,
        ),
        name=name,
    )(where, features, *arrays)


CHUNKS = (
    ((0, 0), (0, 1), (0, 3), (1, 0)),
    ((0, 2), (1, 1), (1, 3)),
    ((1, 2),),
)


def pair_kernel(where_ref, *refs):
    parts, outs, all_ref = refs[:6], refs[6:18], refs[18]
    z, group = where_ref[1], where_ref[2]
    for i, chunks in enumerate(CHUNKS):
        keep_ref, got_ref = parts[2 * i : 2 * i + 2]
        for m, (other, dx) in enumerate(chunks):
            chain = group if other == 0 else 1 - group
            for high in range(2):
                slot = lax.rem(2 * dx + high - z + 8, 8)
                both = keep_ref[2 * m + high].astype(F32) + got_ref[2 * m + high].astype(F32)
                all_ref[chain * 8 + slot] = both.astype(BF)
    half = BLK // 2
    for chain in range(2):
        lo, hi, s3, s2, s1, s0 = outs[6 * chain : 6 * chain + 6]
        lo[...] = all_ref[8 * chain + 4, :half]
        hi[...] = all_ref[8 * chain + 4, half:]
        for ref, d in ((s3, 3), (s2, 2), (s1, 1)):
            ref[0] = all_ref[8 * chain + d]
            ref[1] = all_ref[8 * chain + 8 - d]
        s0[...] = all_ref[8 * chain]


def add_half_kernel(slots_ref, lo_ref, hi_ref, up_ref, down_ref):
    half = BLK // 2
    up_ref[:half] = (slots_ref[0, :half].astype(F32) + lo_ref[...].astype(F32)).astype(BF)
    up_ref[half:] = slots_ref[0, half:]
    down_ref[:half] = slots_ref[1, :half]
    down_ref[half:] = (slots_ref[1, half:].astype(F32) + hi_ref[...].astype(F32)).astype(BF)


def add_kernel(slots_ref, got_up_ref, got_down_ref, up_ref, down_ref):
    up_ref[...] = (slots_ref[0].astype(F32) + got_up_ref[...].astype(F32)).astype(BF)
    down_ref[...] = (slots_ref[1].astype(F32) + got_down_ref[...].astype(F32)).astype(BF)


def end_kernel(slot_ref, got_up_ref, got_down_ref, out_ref):
    total = slot_ref[...].astype(F32) + got_up_ref[...].astype(F32)
    out_ref[...] = (total + got_down_ref[...].astype(F32)).astype(BF)


def sum_kernel(a_ref, b_ref, out_ref):
    out_ref[...] = (a_ref[...].astype(F32) + b_ref[...].astype(F32)).astype(BF)


def small_call(body, out_shape, *args, name, first=VMEM_SPEC, scratch=()):
    many = isinstance(out_shape, tuple)
    return pl.pallas_call(
        body,
        out_shape=out_shape,
        in_specs=[first] + [VMEM_SPEC] * (len(args) - 1),
        out_specs=tuple([VMEM_SPEC] * len(out_shape)) if many else VMEM_SPEC,
        scratch_shapes=scratch,
        compiler_params=PARAMS,
        cost_estimate=pl.CostEstimate(
            flops=1 << 20, bytes_accessed=2 * 1024 * 1024, transcendentals=0
        ),
        name=name,
    )(*args)


def reduce_z(where, *parts):
    block = jax.ShapeDtypeStruct((BLK, BLK), BF)
    half = jax.ShapeDtypeStruct((BLK // 2, BLK), BF)
    both = jax.ShapeDtypeStruct((2, BLK, BLK), BF)
    outs = small_call(
        pair_kernel,
        (half, half, both, both, both, block) * 2,
        where,
        *parts,
        name="pair",
        first=SMEM_SPEC,
        scratch=[pltpu.VMEM((16, BLK, BLK), BF)],
    )
    chains = [outs[:6], outs[6:]]
    moving = [(c[0], c[1]) for c in chains]
    for hop in range(4):
        for i, chain in enumerate(chains):
            up, down = shift(moving[i][0], "z", 1), shift(moving[i][1], "z", -1)
            if hop == 0:
                moving[i] = small_call(add_half_kernel, (block, block), chain[2], up, down, name="add_half")
            elif hop < 3:
                moving[i] = small_call(add_kernel, (block, block), chain[2 + hop], up, down, name="add")
            else:
                moving[i] = small_call(end_kernel, block, chain[5], up, down, name="end")
    return moving


def to_owner(block):
    pairs = []
    for g in range(2):
        for z in range(8):
            for core in range(2):
                for ylo in range(2):
                    for x in range(4):
                        owner = flat(ylo, 2 * x + z % 2, core, ylo ^ g, (x + z // 2) % 4)
                        pairs.append((flat(g, z, core, ylo, x), owner))
    return lax.ppermute(block, AXES, pairs)


def step(total, scale, master, first, second):
    gradient = total.T * scale
    first = beta_one * first + (1.0 - beta_one) * gradient
    second = beta_two * second + (1.0 - beta_two) * gradient * gradient
    way = first / bias_first / (jnp.sqrt(second / bias_second) + adam_eps) + decay_rate * master
    return master - learn_rate * way, first, second


def update_kernel(scale, summed_ref, w_ref, m_ref, v_ref, wo, mo, vo, ro):
    master, first, second = step(
        summed_ref[...].astype(F32), scale, w_ref[...], m_ref[...], v_ref[...]
    )
    wo[...] = master
    mo[...] = first
    vo[...] = second
    ro[...] = master.astype(BF)


def place_kernel(layout, first_source, where_ref, *refs):
    out_ref, sem = refs[-2:]
    core, z, group = (where_ref[i] for i in range(3))
    copies = []
    for ref, blocks in zip(refs[first_source:], layout):
        at = 0
        for flip_g, dz, flip_c, first, rows in blocks:
            g = 1 - group if flip_g else group
            c = 1 - core if flip_c else core
            zz = lax.rem(z + dz + 8, 8)
            row = pl.multiple_of((g * 16 + zz * 2 + c) * BLK + first, BLK // 2)
            copies.append(
                pltpu.make_async_copy(
                    ref.at[pl.ds(at, rows), :], out_ref.at[pl.ds(row, rows), :], sem.at[len(copies)]
                )
            )
            at += rows
    for copy in copies:
        copy.start()
    for copy in copies:
        copy.wait()


def gather_rows(where, own):
    half = BLK // 2
    other = shift(own, "group", 1)
    up, down = [own], [own]
    other_up, other_down = [other], [other]
    for _ in range(3):
        up.append(shift(up[-1], "z", 1))
        down.append(shift(down[-1], "z", -1))
        other_up.append(shift(other_up[-1], "z", 1))
        other_down.append(shift(other_down[-1], "z", -1))
    lo = shift(up[3][:half], "z", 1)
    hi = shift(down[3][half:], "z", -1)
    other_lo = shift(other_up[3][:half], "z", 1)
    other_hi = shift(other_down[3][half:], "z", -1)
    sets = [
        [(own, 0, 0, 0, BLK), (up[1], 0, -1, 0, BLK), (down[1], 0, 1, 0, BLK), (other, 1, 0, 0, BLK)],
        [
            (up[2], 0, -2, 0, BLK),
            (down[2], 0, 2, 0, BLK),
            (other_up[1], 1, -1, 0, BLK),
            (other_down[1], 1, 1, 0, BLK),
        ],
        [
            (up[3], 0, -3, 0, BLK),
            (down[3], 0, 3, 0, BLK),
            (other_up[2], 1, -2, 0, BLK),
            (other_down[2], 1, 2, 0, BLK),
        ],
        [
            (lo, 0, 4, 0, half),
            (hi, 0, 4, half, half),
            (other_up[3], 1, -3, 0, BLK),
            (other_down[3], 1, 3, 0, BLK),
            (other_lo, 1, 4, 0, half),
            (other_hi, 1, 4, half, half),
        ],
    ]
    early, late = [], []
    for i, blocks in enumerate(sets):
        both = jnp.concatenate([b[0] for b in blocks])
        for flip in range(2):
            layout = tuple((g, dz, flip, first, rows) for _, g, dz, first, rows in blocks)
            source = (shift(both, "core", 1) if flip else both, layout)
            (late if i == 3 else early).append(source)
    return place(where, late, place(where, early, None))


def place(where, sources, filled):
    given = [] if filled is None else [filled]
    return pl.pallas_call(
        functools.partial(place_kernel, tuple(b for _, b in sources), len(given)),
        out_shape=jax.ShapeDtypeStruct((32 * BLK, BLK), BF),
        in_specs=[SMEM_SPEC] + [ANY_SPEC] * (len(given) + len(sources)),
        out_specs=ANY_SPEC,
        scratch_shapes=[pltpu.SemaphoreType.DMA((sum(len(b) for _, b in sources),))],
        input_output_aliases={1: 0} if given else {},
        compiler_params=PARAMS,
        cost_estimate=pl.CostEstimate(flops=0, bytes_accessed=4 * 1024 * 1024, transcendentals=0),
        name="place_late" if given else "place_early",
    )(where, *given, *[s for s, _ in sources])


def local(
    features,
    cotangent,
    master,
    first_moment,
    second_moment,
    queries,
    key_cache,
    value_cache,
    new_kv,
    lengths,
):
    tokens = features.shape[0]
    scale = float(tokens * 32) ** (-0.5)
    where = jnp.stack(
        [lax.axis_index(a) for a in ("core", "z", "group")]
    ).astype(jnp.int32)
    half = tokens // 2
    block = jax.ShapeDtypeStruct((BLK, BLK), BF)

    xm = shift(cotangent, "x", 1)
    xp = shift(cotangent, "x", -1)
    mate_lo = shift(cotangent[:half], "ylo", 1)
    mate_hi = shift(cotangent[half:], "ylo", 1)
    bm_lo = shift(mate_lo, "x", 1)
    bp_hi = shift(mate_hi, "x", -1)
    got_mate = shift(jnp.concatenate([xm[half:], xp[:half]]), "ylo", 1)
    far_lo = shift(xm[:half], "x", 1)
    far_hi = shift(xp[half:], "x", -1)
    bf_lo = shift(bm_lo, "x", 1)
    bf_hi = shift(bp_hi, "x", -1)
    attended = attend(queries, key_cache, value_cache, new_kv, lengths)

    features_a = after(features, attended)
    keep_a, send_a = product(
        where,
        features_a,
        [cotangent, xp, xm, mate_lo, mate_hi],
        (((0, 0, tokens),), ((1, 0, tokens),), ((2, 0, tokens),), ((3, 0, half), (4, 0, half))),
        "product_a",
    )
    core_a = shift(send_a, "core", 1)
    features_b = after(features, keep_a)
    keep_b, send_b = product(
        where,
        features_b,
        [far_lo, far_hi, got_mate, bp_hi, bm_lo],
        (
            ((0, 0, half), (1, 0, half)),
            ((2, half, half), (3, 0, half)),
            ((4, 0, half), (2, 0, half)),
        ),
        "product_b",
    )
    features_c = after(features, keep_b)
    keep_c, send_c = product(
        where, features_c, [bf_lo, bf_hi], (((0, 0, half), (1, 0, half)),), "product_c"
    )
    core_b = shift(after(send_b, keep_c), "core", 1)
    core_c = shift(send_c, "core", 1)
    even, odd = reduce_z(where, keep_a, core_a, keep_b, core_b, keep_c, core_c)
    summed = small_call(sum_kernel, block, even, shift(odd, "group", 1), name="sum")

    out32 = jax.ShapeDtypeStruct((BLK, BLK), F32)
    master_out, first_out, second_out, own = small_call(
        functools.partial(update_kernel, scale),
        (out32, out32, out32, block),
        to_owner(summed),
        master,
        first_moment,
        second_moment,
        name="update",
    )
    rollout = gather_rows(where, own)
    return (master_out, first_out, second_out, rollout, attended)


def solution(mesh):
    fine = Mesh(mesh.devices.reshape(SIZES), AXES)
    rows, cols = ("group", "z", "core"), ("ylo", "x")
    return jax.shard_map(
        local,
        mesh=fine,
        in_specs=(
            P(rows, cols),
            P(rows, cols),
            P(rows, cols),
            P(rows, cols),
            P(rows, cols),
            P(rows, cols),
            P(rows, None, cols),
            P(rows, None, cols),
            P(rows, cols),
            P(rows),
        ),
        out_specs=(
            P(rows, cols),
            P(rows, cols),
            P(rows, cols),
            P(None, cols),
            P(rows, cols),
        ),
        check_vma=False,
    )
```

```python
import functools

import jax
import jax.numpy as jnp
from jax import lax
from jax.experimental import pallas as pl
from jax.experimental.pallas import tpu as pltpu
from jax.sharding import Mesh
from jax.sharding import PartitionSpec as P

QH = 64
KVH = 8
HD = 128
GROUPS = QH // KVH
BLK = 256

beta_one = 0.9
beta_two = 0.95
adam_eps = 1e-08
learn_rate = 0.05
decay_rate = 0.1
bias_first = 1.0 - 0.9**10
bias_second = 1.0 - 0.95**10

AXES = ("group", "z", "core", "ylo", "x")
SIZES = (2, 8, 2, 2, 4)
VMEM_SPEC = pl.BlockSpec(memory_space=pltpu.VMEM)
SMEM_SPEC = pl.BlockSpec(memory_space=pltpu.SMEM)
ANY_SPEC = pl.BlockSpec(memory_space=pl.ANY)
MIB = 1024 * 1024


def params(mib):
    return pltpu.CompilerParams(vmem_limit_bytes=mib * MIB)


BF = jnp.bfloat16
F32 = jnp.float32


def shift(value, axis, by):
    size = SIZES[AXES.index(axis)]
    return lax.ppermute(value, axis, [(i, (i + by) % size) for i in range(size)])


def after(value, *marks):
    return lax.optimization_barrier((value, *marks))[0]


def flat(g, z, core, ylo, x):
    return (((g * 8 + z) * 2 + core) * 2 + ylo) * 4 + x


def attend_kernel(lengths_ref, q_ref, k_ref, v_ref, fresh_ref, out_ref):
    scale = HD ** (-0.5)
    rows, span, _ = k_ref.shape
    for r in range(rows):
        q = q_ref[r]
        scores = (
            lax.dot_general(q, k_ref[r], (((1,), (1,)), ((), ())), preferred_element_type=F32)
            * scale
        )
        at = lax.broadcasted_iota(jnp.int32, (GROUPS, span), 1)
        scores = jnp.where(at < lengths_ref[r], scores, -jnp.inf)
        fresh = fresh_ref[r : r + 1, :]
        new_k = fresh[:, :HD].astype(F32)
        new_v = fresh[:, HD:].astype(F32)
        own = jnp.sum(q.astype(F32) * new_k, axis=-1, keepdims=True) * scale
        top = jnp.maximum(jnp.max(scores, axis=-1, keepdims=True), own)
        expo = jnp.exp(scores - top)
        own_expo = jnp.exp(own - top)
        total = jnp.sum(expo, axis=-1, keepdims=True) + own_expo
        weights = (expo / total).astype(BF)
        own_weight = (own_expo / total).astype(BF).astype(F32)
        mixed = jnp.dot(weights, v_ref[r], preferred_element_type=F32)
        out_ref[r] = (mixed + own_weight * new_v).astype(BF)


def attend(queries, key_cache, value_cache, new_kv, lengths):
    rows = queries.shape[0]
    span = key_cache.shape[1]
    out = pl.pallas_call(
        attend_kernel,
        out_shape=jax.ShapeDtypeStruct((rows, GROUPS, HD), BF),
        in_specs=[SMEM_SPEC] + [VMEM_SPEC] * 4,
        out_specs=VMEM_SPEC,
        compiler_params=params(8),
        cost_estimate=pl.CostEstimate(
            flops=4 * rows * GROUPS * span * HD,
            bytes_accessed=4 * rows * span * HD,
            transcendentals=rows * GROUPS * span,
        ),
        name="attend",
    )(lengths, queries.reshape(rows, GROUPS, HD), key_cache, value_cache, new_kv)
    return out.reshape(rows, GROUPS * HD)


def product_kernel(chunks, where_ref, f_ref, *refs):
    keep_ref, send_ref = refs[-2:]
    core = where_ref[0]
    for m, pieces in enumerate(chunks):
        for high in range(2):
            for parity, out_ref in ((core, keep_ref), (1 - core, send_ref)):
                cols = pl.ds(pl.multiple_of((2 * high + parity) * BLK, BLK), BLK)
                total = jnp.zeros((BLK, BLK), F32)
                row = 0
                for i, start, count in pieces:
                    total += lax.dot_general(
                        refs[i][start : start + count],
                        f_ref[row : row + count, cols],
                        (((0,), (0,)), ((), ())),
                        preferred_element_type=F32,
                    )
                    row += count
                out_ref[2 * m + high] = total.astype(BF)


def product(where, features, arrays, chunks, name):
    shape = jax.ShapeDtypeStruct((2 * len(chunks), BLK, BLK), BF)
    return pl.pallas_call(
        functools.partial(product_kernel, chunks),
        out_shape=(shape, shape),
        in_specs=[SMEM_SPEC] + [VMEM_SPEC] * (1 + len(arrays)),
        out_specs=(VMEM_SPEC, VMEM_SPEC),
        compiler_params=params(14),
        cost_estimate=pl.CostEstimate(
            flops=2 * 2048 * 1024 * 256 * len(chunks),
            bytes_accessed=10 * 1024 * 1024,
            transcendentals=0,
        ),
        name=name,
    )(where, features, *arrays)


CHUNKS = (
    ((0, 0), (0, 1), (0, 3), (1, 0)),
    ((0, 2), (1, 1), (1, 3)),
    ((1, 2),),
)


def pair_kernel(where_ref, *refs):
    parts, outs, all_ref = refs[:6], refs[6:18], refs[18]
    z, group = where_ref[1], where_ref[2]
    for i, chunks in enumerate(CHUNKS):
        keep_ref, got_ref = parts[2 * i : 2 * i + 2]
        for m, (other, dx) in enumerate(chunks):
            chain = group if other == 0 else 1 - group
            for high in range(2):
                slot = lax.rem(2 * dx + high - z + 8, 8)
                both = keep_ref[2 * m + high].astype(F32) + got_ref[2 * m + high].astype(F32)
                all_ref[chain * 8 + slot] = both.astype(BF)
    for chain in range(2):
        s4, added, plain, s2, s1, s0 = outs[6 * chain : 6 * chain + 6]
        s4[...] = all_ref[8 * chain + 4]
        added[...] = all_ref[8 * chain + (5 if chain else 3)]
        plain[...] = all_ref[8 * chain + (3 if chain else 5)]
        for ref, d in ((s2, 2), (s1, 1)):
            ref[0] = all_ref[8 * chain + d]
            ref[1] = all_ref[8 * chain + 8 - d]
        s0[...] = all_ref[8 * chain]


def add_one_kernel(slot_ref, got_ref, out_ref):
    out_ref[...] = (slot_ref[...].astype(F32) + got_ref[...].astype(F32)).astype(BF)


def add_kernel(slots_ref, got_up_ref, got_down_ref, up_ref, down_ref):
    up_ref[...] = (slots_ref[0].astype(F32) + got_up_ref[...].astype(F32)).astype(BF)
    down_ref[...] = (slots_ref[1].astype(F32) + got_down_ref[...].astype(F32)).astype(BF)


def end_kernel(slot_ref, got_up_ref, got_down_ref, out_ref):
    total = slot_ref[...].astype(F32) + got_up_ref[...].astype(F32)
    out_ref[...] = (total + got_down_ref[...].astype(F32)).astype(BF)


def sum_kernel(a_ref, b_ref, out_ref):
    out_ref[...] = (a_ref[...].astype(F32) + b_ref[...].astype(F32)).astype(BF)


def small_call(body, out_shape, *args, name, first=VMEM_SPEC, scratch=(), mib=6):
    many = isinstance(out_shape, tuple)
    return pl.pallas_call(
        body,
        out_shape=out_shape,
        in_specs=[first] + [VMEM_SPEC] * (len(args) - 1),
        out_specs=tuple([VMEM_SPEC] * len(out_shape)) if many else VMEM_SPEC,
        scratch_shapes=scratch,
        compiler_params=params(mib),
        cost_estimate=pl.CostEstimate(
            flops=1 << 20, bytes_accessed=2 * 1024 * 1024, transcendentals=0
        ),
        name=name,
    )(*args)


def reduce_z(where, *parts):
    block = jax.ShapeDtypeStruct((BLK, BLK), BF)
    both = jax.ShapeDtypeStruct((2, BLK, BLK), BF)
    outs = small_call(
        pair_kernel,
        (block, block, block, both, both, block) * 2,
        where,
        *parts,
        name="pair",
        first=SMEM_SPEC,
        scratch=[pltpu.VMEM((16, BLK, BLK), BF)],
        mib=14,
    )
    moving = []
    for i in range(2):
        s4, added, plain = outs[6 * i : 6 * i + 3]
        ahead = small_call(add_one_kernel, block, added, shift(s4, "z", (1, -1)[i]), name="add_one")
        moving.append((plain, ahead) if i else (ahead, plain))
    for hop in range(3):
        for i in range(2):
            up, down = shift(moving[i][0], "z", 1), shift(moving[i][1], "z", -1)
            slots = outs[6 * i + 3 + hop]
            if hop < 2:
                moving[i] = small_call(add_kernel, (block, block), slots, up, down, name="add")
            else:
                moving[i] = small_call(end_kernel, block, slots, up, down, name="end")
    return moving


def to_owner(block):
    pairs = []
    for g in range(2):
        for z in range(8):
            for core in range(2):
                for ylo in range(2):
                    for x in range(4):
                        owner = flat(ylo, 2 * x + z % 2, core, ylo ^ g, (x + z // 2) % 4)
                        pairs.append((flat(g, z, core, ylo, x), owner))
    return lax.ppermute(block, AXES, pairs)


def step(total, scale, master, first, second):
    gradient = total.T * scale
    first = beta_one * first + (1.0 - beta_one) * gradient
    second = beta_two * second + (1.0 - beta_two) * gradient * gradient
    way = first / bias_first / (jnp.sqrt(second / bias_second) + adam_eps) + decay_rate * master
    return master - learn_rate * way, first, second


def update_kernel(scale, summed_ref, w_ref, m_ref, v_ref, wo, mo, vo, ro):
    master, first, second = step(
        summed_ref[...].astype(F32), scale, w_ref[...], m_ref[...], v_ref[...]
    )
    wo[...] = master
    mo[...] = first
    vo[...] = second
    ro[...] = master.astype(BF)


def place_kernel(layout, first_source, where_ref, *refs):
    out_ref, sem = refs[-2:]
    core, z, group = (where_ref[i] for i in range(3))
    copies = []
    for ref, blocks in zip(refs[first_source:], layout):
        at = 0
        for flip_g, dz, flip_c, first, rows in blocks:
            g = 1 - group if flip_g else group
            c = 1 - core if flip_c else core
            zz = lax.rem(z + dz + 8, 8)
            row = pl.multiple_of((g * 16 + zz * 2 + c) * BLK + first, BLK // 2)
            copies.append(
                pltpu.make_async_copy(
                    ref.at[pl.ds(at, rows), :], out_ref.at[pl.ds(row, rows), :], sem.at[len(copies)]
                )
            )
            at += rows
    for copy in copies:
        copy.start()
    for copy in copies:
        copy.wait()


def gather_rows(where, own):
    other = shift(own, "group", 1)
    up, down = [own], [own]
    other_up, other_down = [other], [other]
    for _ in range(3):
        up.append(shift(up[-1], "z", 1))
        down.append(shift(down[-1], "z", -1))
        other_up.append(shift(other_up[-1], "z", 1))
        other_down.append(shift(other_down[-1], "z", -1))
    def exchanged(*blocks):
        both = jnp.concatenate([b[0] for b in blocks])
        return [
            (
                shift(both, "core", 1) if flip else both,
                tuple((g, dz, flip, 0, BLK) for _, g, dz in blocks),
            )
            for flip in range(2)
        ]

    early = exchanged((own, 0, 0), (up[1], 0, -1), (down[1], 0, 1), (other, 1, 0))
    early += exchanged((up[2], 0, -2), (down[2], 0, 2), (other_up[1], 1, -1), (other_down[1], 1, 1))
    early += exchanged((up[3], 0, -3), (down[3], 0, 3), (other_up[2], 1, -2), (other_down[2], 1, 2))
    placed = place(where, early, None)
    far = shift(up[3], "z", 1)
    other_far = shift(other_down[3], "z", -1)
    late = exchanged((far, 0, 4), (other_up[3], 1, -3), (other_down[3], 1, 3), (other_far, 1, 4))
    return place(where, late, placed)


def place(where, sources, filled):
    given = [] if filled is None else [filled]
    return pl.pallas_call(
        functools.partial(place_kernel, tuple(b for _, b in sources), len(given)),
        out_shape=jax.ShapeDtypeStruct((32 * BLK, BLK), BF),
        in_specs=[SMEM_SPEC] + [ANY_SPEC] * (len(given) + len(sources)),
        out_specs=ANY_SPEC,
        scratch_shapes=[pltpu.SemaphoreType.DMA((sum(len(b) for _, b in sources),))],
        input_output_aliases={1: 0} if given else {},
        compiler_params=params(4),
        cost_estimate=pl.CostEstimate(flops=0, bytes_accessed=4 * 1024 * 1024, transcendentals=0),
        name="place_late" if given else "place_early",
    )(where, *given, *[s for s, _ in sources])


def local(
    features,
    cotangent,
    master,
    first_moment,
    second_moment,
    queries,
    key_cache,
    value_cache,
    new_kv,
    lengths,
):
    tokens = features.shape[0]
    scale = float(tokens * 32) ** (-0.5)
    where = jnp.stack(
        [lax.axis_index(a) for a in ("core", "z", "group")]
    ).astype(jnp.int32)
    half = tokens // 2
    block = jax.ShapeDtypeStruct((BLK, BLK), BF)

    own_lo, own_hi = cotangent[:half], cotangent[half:]
    xm_lo = shift(own_lo, "x", 1)
    xp_hi = shift(own_hi, "x", -1)
    xm_hi = shift(own_hi, "x", 1)
    xp_lo = shift(own_lo, "x", -1)
    mate = shift(cotangent, "ylo", 1)
    far_lo = shift(xm_lo, "x", 1)
    far_hi = shift(xp_hi, "x", -1)
    bm_lo = shift(mate[:half], "x", 1)
    bp_hi = shift(mate[half:], "x", -1)
    got_mate = shift(jnp.concatenate([xm_hi, xp_lo]), "ylo", 1)
    bf_lo = shift(bm_lo, "x", 1)
    bf_hi = shift(bp_hi, "x", -1)
    attended = attend(queries, key_cache, value_cache, new_kv, lengths)

    features_a = after(features, attended)
    keep_a, send_a = product(
        where,
        features_a,
        [cotangent, xp_lo, xp_hi, xm_lo, xm_hi, mate],
        (
            ((0, 0, tokens),),
            ((1, 0, half), (2, 0, half)),
            ((3, 0, half), (4, 0, half)),
            ((5, 0, tokens),),
        ),
        "product_a",
    )
    core_a = shift(send_a, "core", 1)
    features_b = after(features, keep_a)
    keep_b, send_b = product(
        where,
        features_b,
        [far_lo, far_hi, got_mate, bp_hi, bm_lo],
        (
            ((0, 0, half), (1, 0, half)),
            ((2, half, half), (3, 0, half)),
            ((4, 0, half), (2, 0, half)),
        ),
        "product_b",
    )
    features_c = after(features, keep_b)
    keep_c, send_c = product(
        where, features_c, [bf_lo, bf_hi], (((0, 0, half), (1, 0, half)),), "product_c"
    )
    core_b = shift(after(send_b, keep_c), "core", 1)
    core_c = shift(send_c, "core", 1)
    even, odd = reduce_z(where, keep_a, core_a, keep_b, core_b, keep_c, core_c)
    summed = small_call(sum_kernel, block, even, shift(odd, "group", 1), name="sum")

    out32 = jax.ShapeDtypeStruct((BLK, BLK), F32)
    master_out, first_out, second_out, own = small_call(
        functools.partial(update_kernel, scale),
        (out32, out32, out32, block),
        to_owner(summed),
        master,
        first_moment,
        second_moment,
        name="update",
    )
    rollout = gather_rows(where, own)
    return (master_out, first_out, second_out, rollout, attended)


def solution(mesh):
    fine = Mesh(mesh.devices.reshape(SIZES), AXES)
    rows, cols = ("group", "z", "core"), ("ylo", "x")
    return jax.shard_map(
        local,
        mesh=fine,
        in_specs=(
            P(rows, cols),
            P(rows, cols),
            P(rows, cols),
            P(rows, cols),
            P(rows, cols),
            P(rows, cols),
            P(rows, None, cols),
            P(rows, None, cols),
            P(rows, cols),
            P(rows),
        ),
        out_specs=(
            P(rows, cols),
            P(rows, cols),
            P(rows, cols),
            P(None, cols),
            P(rows, cols),
        ),
        check_vma=False,
    )
```

```python
import functools

import jax
import jax.numpy as jnp
from jax import lax
from jax.experimental import pallas as pl
from jax.experimental.pallas import tpu as pltpu
from jax.sharding import Mesh
from jax.sharding import PartitionSpec as P

QH = 64
KVH = 8
HD = 128
GROUPS = QH // KVH
BLK = 256

beta_one = 0.9
beta_two = 0.95
adam_eps = 1e-08
learn_rate = 0.05
decay_rate = 0.1
bias_first = 1.0 - 0.9**10
bias_second = 1.0 - 0.95**10

AXES = ("group", "z", "core", "ylo", "x")
SIZES = (2, 8, 2, 2, 4)
VMEM_SPEC = pl.BlockSpec(memory_space=pltpu.VMEM)
SMEM_SPEC = pl.BlockSpec(memory_space=pltpu.SMEM)
ANY_SPEC = pl.BlockSpec(memory_space=pl.ANY)
MIB = 1024 * 1024


def params(mib):
    return pltpu.CompilerParams(vmem_limit_bytes=mib * MIB)


BF = jnp.bfloat16
F32 = jnp.float32


def shift(value, axis, by):
    size = SIZES[AXES.index(axis)]
    return lax.ppermute(value, axis, [(i, (i + by) % size) for i in range(size)])


def after(value, *marks):
    return lax.optimization_barrier((value, *marks))[0]


def flat(g, z, core, ylo, x):
    return (((g * 8 + z) * 2 + core) * 2 + ylo) * 4 + x


def attend_kernel(lengths_ref, q_ref, k_ref, v_ref, fresh_ref, out_ref):
    scale = HD ** (-0.5)
    rows, span, _ = k_ref.shape
    for r in range(rows):
        q = q_ref[r]
        scores = (
            lax.dot_general(q, k_ref[r], (((1,), (1,)), ((), ())), preferred_element_type=F32)
            * scale
        )
        at = lax.broadcasted_iota(jnp.int32, (GROUPS, span), 1)
        scores = jnp.where(at < lengths_ref[r], scores, -jnp.inf)
        fresh = fresh_ref[r : r + 1, :]
        new_k = fresh[:, :HD].astype(F32)
        new_v = fresh[:, HD:].astype(F32)
        own = jnp.sum(q.astype(F32) * new_k, axis=-1, keepdims=True) * scale
        top = jnp.maximum(jnp.max(scores, axis=-1, keepdims=True), own)
        expo = jnp.exp(scores - top)
        own_expo = jnp.exp(own - top)
        total = jnp.sum(expo, axis=-1, keepdims=True) + own_expo
        weights = (expo / total).astype(BF)
        own_weight = (own_expo / total).astype(BF).astype(F32)
        mixed = jnp.dot(weights, v_ref[r], preferred_element_type=F32)
        out_ref[r] = (mixed + own_weight * new_v).astype(BF)


def attend(queries, key_cache, value_cache, new_kv, lengths):
    rows = queries.shape[0]
    span = key_cache.shape[1]
    out = pl.pallas_call(
        attend_kernel,
        out_shape=jax.ShapeDtypeStruct((rows, GROUPS, HD), BF),
        in_specs=[SMEM_SPEC] + [VMEM_SPEC] * 4,
        out_specs=VMEM_SPEC,
        compiler_params=params(8),
        cost_estimate=pl.CostEstimate(
            flops=4 * rows * GROUPS * span * HD,
            bytes_accessed=4 * rows * span * HD,
            transcendentals=rows * GROUPS * span,
        ),
        name="attend",
    )(lengths, queries.reshape(rows, GROUPS, HD), key_cache, value_cache, new_kv)
    return out.reshape(rows, GROUPS * HD)


def product_kernel(chunks, where_ref, f_ref, *refs):
    keep_ref, send_ref = refs[-2:]
    core = where_ref[0]
    for m, pieces in enumerate(chunks):
        for high in range(2):
            for parity, out_ref in ((core, keep_ref), (1 - core, send_ref)):
                cols = pl.ds(pl.multiple_of((2 * high + parity) * BLK, BLK), BLK)
                total = jnp.zeros((BLK, BLK), F32)
                row = 0
                for i, start, count in pieces:
                    total += lax.dot_general(
                        refs[i][start : start + count],
                        f_ref[row : row + count, cols],
                        (((0,), (0,)), ((), ())),
                        preferred_element_type=F32,
                    )
                    row += count
                out_ref[2 * m + high] = total.astype(BF)


def product(where, features, arrays, chunks, name):
    shape = jax.ShapeDtypeStruct((2 * len(chunks), BLK, BLK), BF)
    return pl.pallas_call(
        functools.partial(product_kernel, chunks),
        out_shape=(shape, shape),
        in_specs=[SMEM_SPEC] + [VMEM_SPEC] * (1 + len(arrays)),
        out_specs=(VMEM_SPEC, VMEM_SPEC),
        compiler_params=params(14),
        cost_estimate=pl.CostEstimate(
            flops=2 * 2048 * 1024 * 256 * len(chunks),
            bytes_accessed=10 * 1024 * 1024,
            transcendentals=0,
        ),
        name=name,
    )(where, features, *arrays)


CHUNKS = (
    ((0, 0),),
    ((0, 1), (0, 3), (1, 0)),
    ((0, 2), (1, 1), (1, 3)),
    ((1, 2),),
)


def pair_kernel(where_ref, *refs):
    parts, outs, all_ref = refs[:8], refs[8:20], refs[20]
    z, group = where_ref[1], where_ref[2]
    for i, chunks in enumerate(CHUNKS):
        keep_ref, got_ref = parts[2 * i : 2 * i + 2]
        for m, (other, dx) in enumerate(chunks):
            chain = group if other == 0 else 1 - group
            for high in range(2):
                slot = lax.rem(2 * dx + high - z + 8, 8)
                both = keep_ref[2 * m + high].astype(F32) + got_ref[2 * m + high].astype(F32)
                all_ref[chain * 8 + slot] = both.astype(BF)
    for chain in range(2):
        s4, added, plain, s2, s1, s0 = outs[6 * chain : 6 * chain + 6]
        s4[...] = all_ref[8 * chain + 4]
        added[...] = all_ref[8 * chain + (5 if chain else 3)]
        plain[...] = all_ref[8 * chain + (3 if chain else 5)]
        for ref, d in ((s2, 2), (s1, 1)):
            ref[0] = all_ref[8 * chain + d]
            ref[1] = all_ref[8 * chain + 8 - d]
        s0[...] = all_ref[8 * chain]


def add_one_kernel(slot_ref, got_ref, out_ref):
    out_ref[...] = (slot_ref[...].astype(F32) + got_ref[...].astype(F32)).astype(BF)


def add_kernel(slots_ref, got_up_ref, got_down_ref, up_ref, down_ref):
    up_ref[...] = (slots_ref[0].astype(F32) + got_up_ref[...].astype(F32)).astype(BF)
    down_ref[...] = (slots_ref[1].astype(F32) + got_down_ref[...].astype(F32)).astype(BF)


def end_kernel(slot_ref, got_up_ref, got_down_ref, out_ref):
    total = slot_ref[...].astype(F32) + got_up_ref[...].astype(F32)
    out_ref[...] = (total + got_down_ref[...].astype(F32)).astype(BF)


def sum_kernel(a_ref, b_ref, out_ref):
    out_ref[...] = (a_ref[...].astype(F32) + b_ref[...].astype(F32)).astype(BF)


def small_call(body, out_shape, *args, name, first=VMEM_SPEC, scratch=(), mib=6):
    many = isinstance(out_shape, tuple)
    return pl.pallas_call(
        body,
        out_shape=out_shape,
        in_specs=[first] + [VMEM_SPEC] * (len(args) - 1),
        out_specs=tuple([VMEM_SPEC] * len(out_shape)) if many else VMEM_SPEC,
        scratch_shapes=scratch,
        compiler_params=params(mib),
        cost_estimate=pl.CostEstimate(
            flops=1 << 20, bytes_accessed=2 * 1024 * 1024, transcendentals=0
        ),
        name=name,
    )(*args)


def reduce_z(where, *parts):
    block = jax.ShapeDtypeStruct((BLK, BLK), BF)
    both = jax.ShapeDtypeStruct((2, BLK, BLK), BF)
    outs = small_call(
        pair_kernel,
        (block, block, block, both, both, block) * 2,
        where,
        *parts,
        name="pair",
        first=SMEM_SPEC,
        scratch=[pltpu.VMEM((16, BLK, BLK), BF)],
        mib=14,
    )
    moving = []
    for i in range(2):
        s4, added, plain = outs[6 * i : 6 * i + 3]
        ahead = small_call(add_one_kernel, block, added, shift(s4, "z", (1, -1)[i]), name="add_one")
        moving.append((plain, ahead) if i else (ahead, plain))
    for hop in range(3):
        for i in range(2):
            up, down = shift(moving[i][0], "z", 1), shift(moving[i][1], "z", -1)
            slots = outs[6 * i + 3 + hop]
            if hop < 2:
                moving[i] = small_call(add_kernel, (block, block), slots, up, down, name="add")
            else:
                moving[i] = small_call(end_kernel, block, slots, up, down, name="end")
    return moving


def to_owner(block):
    pairs = []
    for g in range(2):
        for z in range(8):
            for core in range(2):
                for ylo in range(2):
                    for x in range(4):
                        owner = flat(ylo, 2 * x + z % 2, core, ylo ^ g, (x + z // 2) % 4)
                        pairs.append((flat(g, z, core, ylo, x), owner))
    return lax.ppermute(block, AXES, pairs)


def step(total, scale, master, first, second):
    gradient = total.T * scale
    first = beta_one * first + (1.0 - beta_one) * gradient
    second = beta_two * second + (1.0 - beta_two) * gradient * gradient
    way = first / bias_first / (jnp.sqrt(second / bias_second) + adam_eps) + decay_rate * master
    return master - learn_rate * way, first, second


def update_kernel(scale, summed_ref, w_ref, m_ref, v_ref, wo, mo, vo, ro):
    master, first, second = step(
        summed_ref[...].astype(F32), scale, w_ref[...], m_ref[...], v_ref[...]
    )
    wo[...] = master
    mo[...] = first
    vo[...] = second
    ro[...] = master.astype(BF)


def place_kernel(layout, first_source, where_ref, *refs):
    out_ref, sem = refs[-2:]
    core, z, group = (where_ref[i] for i in range(3))
    copies = []
    for ref, blocks in zip(refs[first_source:], layout):
        at = 0
        for flip_g, dz, flip_c, first, rows in blocks:
            g = 1 - group if flip_g else group
            c = 1 - core if flip_c else core
            zz = lax.rem(z + dz + 8, 8)
            row = pl.multiple_of((g * 16 + zz * 2 + c) * BLK + first, BLK // 2)
            copies.append(
                pltpu.make_async_copy(
                    ref.at[pl.ds(at, rows), :], out_ref.at[pl.ds(row, rows), :], sem.at[len(copies)]
                )
            )
            at += rows
    for copy in copies:
        copy.start()
    for copy in copies:
        copy.wait()


def gather_rows(where, own):
    other = shift(own, "group", 1)
    up, down = [own], [own]
    other_up, other_down = [other], [other]
    for _ in range(3):
        up.append(shift(up[-1], "z", 1))
        down.append(shift(down[-1], "z", -1))
        other_up.append(shift(other_up[-1], "z", 1))
        other_down.append(shift(other_down[-1], "z", -1))
    def exchanged(*blocks):
        both = jnp.concatenate([b[0] for b in blocks])
        return [
            (
                shift(both, "core", 1) if flip else both,
                tuple((g, dz, flip, 0, BLK) for _, g, dz in blocks),
            )
            for flip in range(2)
        ]

    early = exchanged((own, 0, 0), (up[1], 0, -1), (down[1], 0, 1), (other, 1, 0))
    early += exchanged((up[2], 0, -2), (down[2], 0, 2), (other_up[1], 1, -1), (other_down[1], 1, 1))
    early += exchanged((up[3], 0, -3), (down[3], 0, 3), (other_up[2], 1, -2), (other_down[2], 1, 2))
    placed = place(where, early, None)
    far = shift(up[3], "z", 1)
    other_far = shift(other_down[3], "z", -1)
    late = exchanged((far, 0, 4), (other_up[3], 1, -3), (other_down[3], 1, 3), (other_far, 1, 4))
    return place(where, late, placed)


def place(where, sources, filled):
    given = [] if filled is None else [filled]
    return pl.pallas_call(
        functools.partial(place_kernel, tuple(b for _, b in sources), len(given)),
        out_shape=jax.ShapeDtypeStruct((32 * BLK, BLK), BF),
        in_specs=[SMEM_SPEC] + [ANY_SPEC] * (len(given) + len(sources)),
        out_specs=ANY_SPEC,
        scratch_shapes=[pltpu.SemaphoreType.DMA((sum(len(b) for _, b in sources),))],
        input_output_aliases={1: 0} if given else {},
        compiler_params=params(4),
        cost_estimate=pl.CostEstimate(flops=0, bytes_accessed=4 * 1024 * 1024, transcendentals=0),
        name="place_late" if given else "place_early",
    )(where, *given, *[s for s, _ in sources])


def local(
    features,
    cotangent,
    master,
    first_moment,
    second_moment,
    queries,
    key_cache,
    value_cache,
    new_kv,
    lengths,
):
    tokens = features.shape[0]
    scale = float(tokens * 32) ** (-0.5)
    where = jnp.stack(
        [lax.axis_index(a) for a in ("core", "z", "group")]
    ).astype(jnp.int32)
    half = tokens // 2
    block = jax.ShapeDtypeStruct((BLK, BLK), BF)

    own_lo, own_hi = cotangent[:half], cotangent[half:]
    xm_lo = shift(own_lo, "x", 1)
    xp_hi = shift(own_hi, "x", -1)
    xm_hi = shift(own_hi, "x", 1)
    xp_lo = shift(own_lo, "x", -1)
    mate = shift(cotangent, "ylo", 1)
    far_lo = shift(xm_lo, "x", 1)
    far_hi = shift(xp_hi, "x", -1)
    bm_lo = shift(mate[:half], "x", 1)
    bp_hi = shift(mate[half:], "x", -1)
    bf_lo = shift(bm_lo, "x", 1)
    bf_hi = shift(bp_hi, "x", -1)
    attended = attend(queries, key_cache, value_cache, new_kv, lengths)

    keep_own, send_own = product(
        where, features, [cotangent], (((0, 0, tokens),),), "product_own"
    )
    core_own = shift(send_own, "core", 1)
    got_mate = shift(
        jnp.concatenate([after(xm_hi, keep_own, attended), xp_lo]), "ylo", 1
    )
    features_a = after(features, keep_own)
    keep_a, send_a = product(
        where,
        features_a,
        [xp_lo, xp_hi, xm_lo, xm_hi, mate],
        (
            ((0, 0, half), (1, 0, half)),
            ((2, 0, half), (3, 0, half)),
            ((4, 0, tokens),),
        ),
        "product_a",
    )
    core_a = shift(send_a, "core", 1)
    features_b = after(features, keep_a)
    keep_b, send_b = product(
        where,
        features_b,
        [far_lo, far_hi, got_mate, bp_hi, bm_lo],
        (
            ((0, 0, half), (1, 0, half)),
            ((2, half, half), (3, 0, half)),
            ((4, 0, half), (2, 0, half)),
        ),
        "product_b",
    )
    features_c = after(features, keep_b)
    keep_c, send_c = product(
        where, features_c, [bf_lo, bf_hi], (((0, 0, half), (1, 0, half)),), "product_c"
    )
    core_b = shift(after(send_b, keep_c), "core", 1)
    core_c = shift(send_c, "core", 1)
    even, odd = reduce_z(
        where, keep_own, core_own, keep_a, core_a, keep_b, core_b, keep_c, core_c
    )
    summed = small_call(sum_kernel, block, even, shift(odd, "group", 1), name="sum")

    out32 = jax.ShapeDtypeStruct((BLK, BLK), F32)
    master_out, first_out, second_out, own = small_call(
        functools.partial(update_kernel, scale),
        (out32, out32, out32, block),
        to_owner(summed),
        master,
        first_moment,
        second_moment,
        name="update",
    )
    rollout = gather_rows(where, own)
    return (master_out, first_out, second_out, rollout, attended)


def solution(mesh):
    fine = Mesh(mesh.devices.reshape(SIZES), AXES)
    rows, cols = ("group", "z", "core"), ("ylo", "x")
    return jax.shard_map(
        local,
        mesh=fine,
        in_specs=(
            P(rows, cols),
            P(rows, cols),
            P(rows, cols),
            P(rows, cols),
            P(rows, cols),
            P(rows, cols),
            P(rows, None, cols),
            P(rows, None, cols),
            P(rows, cols),
            P(rows),
        ),
        out_specs=(
            P(rows, cols),
            P(rows, cols),
            P(rows, cols),
            P(None, cols),
            P(rows, cols),
        ),
        check_vma=False,
    )
```

```python
import functools

import jax
import jax.numpy as jnp
from jax import lax
from jax.experimental import pallas as pl
from jax.experimental.pallas import tpu as pltpu
from jax.sharding import Mesh
from jax.sharding import PartitionSpec as P

QH = 64
KVH = 8
HD = 128
GROUPS = QH // KVH
BLK = 256

beta_one = 0.9
beta_two = 0.95
adam_eps = 1e-08
learn_rate = 0.05
decay_rate = 0.1
bias_first = 1.0 - 0.9**10
bias_second = 1.0 - 0.95**10

AXES = ("group", "z", "core", "ylo", "x")
SIZES = (2, 8, 2, 2, 4)
VMEM_SPEC = pl.BlockSpec(memory_space=pltpu.VMEM)
SMEM_SPEC = pl.BlockSpec(memory_space=pltpu.SMEM)
ANY_SPEC = pl.BlockSpec(memory_space=pl.ANY)
MIB = 1024 * 1024


def params(mib):
    return pltpu.CompilerParams(vmem_limit_bytes=mib * MIB)


BF = jnp.bfloat16
F32 = jnp.float32


def shift(value, axis, by):
    size = SIZES[AXES.index(axis)]
    return lax.ppermute(value, axis, [(i, (i + by) % size) for i in range(size)])


def after(value, *marks):
    return lax.optimization_barrier((value, *marks))[0]


def flat(g, z, core, ylo, x):
    return (((g * 8 + z) * 2 + core) * 2 + ylo) * 4 + x


def attend_kernel(lengths_ref, q_ref, k_ref, v_ref, fresh_ref, out_ref):
    scale = HD ** (-0.5)
    rows, span, _ = k_ref.shape
    for r in range(rows):
        q = q_ref[r]
        scores = (
            lax.dot_general(q, k_ref[r], (((1,), (1,)), ((), ())), preferred_element_type=F32)
            * scale
        )
        at = lax.broadcasted_iota(jnp.int32, (GROUPS, span), 1)
        scores = jnp.where(at < lengths_ref[r], scores, -jnp.inf)
        fresh = fresh_ref[r : r + 1, :]
        new_k = fresh[:, :HD].astype(F32)
        new_v = fresh[:, HD:].astype(F32)
        own = jnp.sum(q.astype(F32) * new_k, axis=-1, keepdims=True) * scale
        top = jnp.maximum(jnp.max(scores, axis=-1, keepdims=True), own)
        expo = jnp.exp(scores - top)
        own_expo = jnp.exp(own - top)
        total = jnp.sum(expo, axis=-1, keepdims=True) + own_expo
        weights = (expo / total).astype(BF)
        own_weight = (own_expo / total).astype(BF).astype(F32)
        mixed = jnp.dot(weights, v_ref[r], preferred_element_type=F32)
        out_ref[r] = (mixed + own_weight * new_v).astype(BF)


def attend(queries, key_cache, value_cache, new_kv, lengths):
    rows = queries.shape[0]
    span = key_cache.shape[1]
    out = pl.pallas_call(
        attend_kernel,
        out_shape=jax.ShapeDtypeStruct((rows, GROUPS, HD), BF),
        in_specs=[SMEM_SPEC] + [VMEM_SPEC] * 4,
        out_specs=VMEM_SPEC,
        compiler_params=params(8),
        cost_estimate=pl.CostEstimate(
            flops=4 * rows * GROUPS * span * HD,
            bytes_accessed=4 * rows * span * HD,
            transcendentals=rows * GROUPS * span,
        ),
        name="attend",
    )(lengths, queries.reshape(rows, GROUPS, HD), key_cache, value_cache, new_kv)
    return out.reshape(rows, GROUPS * HD)


def product_kernel(chunks, where_ref, f_ref, *refs):
    keep_ref, send_ref = refs[-2:]
    core = where_ref[0]
    for m, pieces in enumerate(chunks):
        for high in range(2):
            for parity, out_ref in ((core, keep_ref), (1 - core, send_ref)):
                cols = pl.ds(pl.multiple_of((2 * high + parity) * BLK, BLK), BLK)
                total = jnp.zeros((BLK, BLK), F32)
                row = 0
                for i, start, count in pieces:
                    total += lax.dot_general(
                        refs[i][start : start + count],
                        f_ref[row : row + count, cols],
                        (((0,), (0,)), ((), ())),
                        preferred_element_type=F32,
                    )
                    row += count
                out_ref[2 * m + high] = total.astype(BF)


def product(where, features, arrays, chunks, name):
    shape = jax.ShapeDtypeStruct((2 * len(chunks), BLK, BLK), BF)
    return pl.pallas_call(
        functools.partial(product_kernel, chunks),
        out_shape=(shape, shape),
        in_specs=[SMEM_SPEC] + [VMEM_SPEC] * (1 + len(arrays)),
        out_specs=(VMEM_SPEC, VMEM_SPEC),
        compiler_params=params(14),
        cost_estimate=pl.CostEstimate(
            flops=2 * 2048 * 1024 * 256 * len(chunks),
            bytes_accessed=10 * 1024 * 1024,
            transcendentals=0,
        ),
        name=name,
    )(where, features, *arrays)


CHUNKS = (
    ((0, 0),),
    ((0, 1), (0, 3), (1, 0)),
    ((0, 2), (1, 1), (1, 3)),
    ((1, 2),),
)


def pair_kernel(where_ref, *refs):
    parts, outs, all_ref = refs[:8], refs[8:20], refs[20]
    z, group = where_ref[1], where_ref[2]
    for i, chunks in enumerate(CHUNKS):
        keep_ref, got_ref = parts[2 * i : 2 * i + 2]
        for m, (other, dx) in enumerate(chunks):
            chain = group if other == 0 else 1 - group
            for high in range(2):
                slot = lax.rem(2 * dx + high - z + 8, 8)
                both = keep_ref[2 * m + high].astype(F32) + got_ref[2 * m + high].astype(F32)
                all_ref[chain * 8 + slot] = both.astype(BF)
    for chain in range(2):
        s4, added, plain, s2, s1, s0 = outs[6 * chain : 6 * chain + 6]
        s4[...] = all_ref[8 * chain + 4]
        added[...] = all_ref[8 * chain + (5 if chain else 3)]
        plain[...] = all_ref[8 * chain + (3 if chain else 5)]
        for ref, d in ((s2, 2), (s1, 1)):
            ref[0] = all_ref[8 * chain + d]
            ref[1] = all_ref[8 * chain + 8 - d]
        s0[...] = all_ref[8 * chain]


def add_one_kernel(slot_ref, got_ref, out_ref):
    out_ref[...] = (slot_ref[...].astype(F32) + got_ref[...].astype(F32)).astype(BF)


def add_kernel(slots_ref, got_up_ref, got_down_ref, up_ref, down_ref):
    up_ref[...] = (slots_ref[0].astype(F32) + got_up_ref[...].astype(F32)).astype(BF)
    down_ref[...] = (slots_ref[1].astype(F32) + got_down_ref[...].astype(F32)).astype(BF)


def end_kernel(slot_ref, got_up_ref, got_down_ref, out_ref):
    total = slot_ref[...].astype(F32) + got_up_ref[...].astype(F32)
    out_ref[...] = (total + got_down_ref[...].astype(F32)).astype(BF)


def sum_kernel(a_ref, b_ref, out_ref):
    out_ref[...] = (a_ref[...].astype(F32) + b_ref[...].astype(F32)).astype(BF)


def small_call(body, out_shape, *args, name, first=VMEM_SPEC, scratch=(), mib=6):
    many = isinstance(out_shape, tuple)
    return pl.pallas_call(
        body,
        out_shape=out_shape,
        in_specs=[first] + [VMEM_SPEC] * (len(args) - 1),
        out_specs=tuple([VMEM_SPEC] * len(out_shape)) if many else VMEM_SPEC,
        scratch_shapes=scratch,
        compiler_params=params(mib),
        cost_estimate=pl.CostEstimate(
            flops=1 << 20, bytes_accessed=2 * 1024 * 1024, transcendentals=0
        ),
        name=name,
    )(*args)


def reduce_z(where, *parts):
    block = jax.ShapeDtypeStruct((BLK, BLK), BF)
    both = jax.ShapeDtypeStruct((2, BLK, BLK), BF)
    outs = small_call(
        pair_kernel,
        (block, block, block, both, both, block) * 2,
        where,
        *parts,
        name="pair",
        first=SMEM_SPEC,
        scratch=[pltpu.VMEM((16, BLK, BLK), BF)],
        mib=14,
    )
    moving = []
    for i in range(2):
        s4, added, plain = outs[6 * i : 6 * i + 3]
        ahead = small_call(add_one_kernel, block, added, shift(s4, "z", (1, -1)[i]), name="add_one")
        moving.append((plain, ahead) if i else (ahead, plain))
    for hop in range(3):
        for i in range(2):
            up, down = shift(moving[i][0], "z", 1), shift(moving[i][1], "z", -1)
            slots = outs[6 * i + 3 + hop]
            if hop < 2:
                moving[i] = small_call(add_kernel, (block, block), slots, up, down, name="add")
            else:
                moving[i] = small_call(end_kernel, block, slots, up, down, name="end")
    return moving


def to_owner(block):
    pairs = []
    for g in range(2):
        for z in range(8):
            for core in range(2):
                for ylo in range(2):
                    for x in range(4):
                        owner = flat(ylo, 2 * x + z % 2, core, ylo ^ g, (x + z // 2) % 4)
                        pairs.append((flat(g, z, core, ylo, x), owner))
    return lax.ppermute(block, AXES, pairs)


def step(total, scale, master, first, second):
    gradient = total.T * scale
    first = beta_one * first + (1.0 - beta_one) * gradient
    second = beta_two * second + (1.0 - beta_two) * gradient * gradient
    way = first / bias_first / (jnp.sqrt(second / bias_second) + adam_eps) + decay_rate * master
    return master - learn_rate * way, first, second


def refresh_kernel(scale, summed_ref, w_ref, m_ref, v_ref, ro):
    state = (w_ref[...], m_ref[...], v_ref[...])
    ro[...] = step(summed_ref[...].astype(F32), scale, *state)[0].astype(BF)


def update_kernel(scale, summed_ref, w_ref, m_ref, v_ref, wo, mo, vo):
    master, first, second = step(
        summed_ref[...].astype(F32), scale, w_ref[...], m_ref[...], v_ref[...]
    )
    wo[...] = master
    mo[...] = first
    vo[...] = second


def place_kernel(layout, first_source, where_ref, *refs):
    out_ref, sem = refs[-2:]
    core, z, group = (where_ref[i] for i in range(3))
    copies = []
    for ref, blocks in zip(refs[first_source:], layout):
        at = 0
        for flip_g, dz, flip_c, first, rows in blocks:
            g = 1 - group if flip_g else group
            c = 1 - core if flip_c else core
            zz = lax.rem(z + dz + 8, 8)
            row = pl.multiple_of((g * 16 + zz * 2 + c) * BLK + first, BLK // 2)
            copies.append(
                pltpu.make_async_copy(
                    ref.at[pl.ds(at, rows), :], out_ref.at[pl.ds(row, rows), :], sem.at[len(copies)]
                )
            )
            at += rows
    for copy in copies:
        copy.start()
    for copy in copies:
        copy.wait()


def gather_rows(where, own, mark):
    other = shift(own, "group", 1)
    up, down = [own], [own]
    other_up, other_down = [other], [other]
    for _ in range(3):
        up.append(shift(up[-1], "z", 1))
        down.append(shift(after(down[-1], mark) if len(down) == 2 else down[-1], "z", -1))
        other_up.append(shift(other_up[-1], "z", 1))
        other_down.append(shift(other_down[-1], "z", -1))
    def exchanged(*blocks):
        both = jnp.concatenate([b[0] for b in blocks])
        return [
            (
                shift(both, "core", 1) if flip else both,
                tuple((g, dz, flip, 0, BLK) for _, g, dz in blocks),
            )
            for flip in range(2)
        ]

    early = exchanged((own, 0, 0), (up[1], 0, -1), (down[1], 0, 1), (other, 1, 0))
    early += exchanged((up[2], 0, -2), (down[2], 0, 2), (other_up[1], 1, -1), (other_down[1], 1, 1))
    early += exchanged((up[3], 0, -3), (down[3], 0, 3), (other_up[2], 1, -2), (other_down[2], 1, 2))
    placed = place(where, early, None)
    far = shift(up[3], "z", 1)
    other_far = shift(other_down[3], "z", -1)
    late = exchanged((far, 0, 4), (other_up[3], 1, -3), (other_down[3], 1, 3), (other_far, 1, 4))
    return place(where, late, placed)


def place(where, sources, filled):
    given = [] if filled is None else [filled]
    return pl.pallas_call(
        functools.partial(place_kernel, tuple(b for _, b in sources), len(given)),
        out_shape=jax.ShapeDtypeStruct((32 * BLK, BLK), BF),
        in_specs=[SMEM_SPEC] + [ANY_SPEC] * (len(given) + len(sources)),
        out_specs=ANY_SPEC,
        scratch_shapes=[pltpu.SemaphoreType.DMA((sum(len(b) for _, b in sources),))],
        input_output_aliases={1: 0} if given else {},
        compiler_params=params(4),
        cost_estimate=pl.CostEstimate(flops=0, bytes_accessed=4 * 1024 * 1024, transcendentals=0),
        name="place_late" if given else "place_early",
    )(where, *given, *[s for s, _ in sources])


def local(
    features,
    cotangent,
    master,
    first_moment,
    second_moment,
    queries,
    key_cache,
    value_cache,
    new_kv,
    lengths,
):
    tokens = features.shape[0]
    scale = float(tokens * 32) ** (-0.5)
    where = jnp.stack(
        [lax.axis_index(a) for a in ("core", "z", "group")]
    ).astype(jnp.int32)
    half = tokens // 2
    block = jax.ShapeDtypeStruct((BLK, BLK), BF)

    own_lo, own_hi = cotangent[:half], cotangent[half:]
    xm_lo = shift(own_lo, "x", 1)
    xp_hi = shift(own_hi, "x", -1)
    xm_hi = shift(own_hi, "x", 1)
    xp_lo = shift(own_lo, "x", -1)
    mate = shift(cotangent, "ylo", 1)
    far_lo = shift(xm_lo, "x", 1)
    far_hi = shift(xp_hi, "x", -1)
    bm_lo = shift(mate[:half], "x", 1)
    bp_hi = shift(mate[half:], "x", -1)
    bf_lo = shift(bm_lo, "x", 1)
    bf_hi = shift(bp_hi, "x", -1)
    attended = attend(queries, key_cache, value_cache, new_kv, lengths)

    keep_own, send_own = product(
        where, features, [cotangent], (((0, 0, tokens),),), "product_own"
    )
    core_own = shift(send_own, "core", 1)
    got_mate = shift(
        jnp.concatenate([after(xm_hi, keep_own, attended), xp_lo]), "ylo", 1
    )
    features_a = after(features, keep_own)
    keep_a, send_a = product(
        where,
        features_a,
        [xp_lo, xp_hi, xm_lo, xm_hi, mate],
        (
            ((0, 0, half), (1, 0, half)),
            ((2, 0, half), (3, 0, half)),
            ((4, 0, tokens),),
        ),
        "product_a",
    )
    core_a = shift(send_a, "core", 1)
    features_b = after(features, keep_a)
    keep_b, send_b = product(
        where,
        features_b,
        [far_lo, far_hi, got_mate, bp_hi, bm_lo],
        (
            ((0, 0, half), (1, 0, half)),
            ((2, half, half), (3, 0, half)),
            ((4, 0, half), (2, 0, half)),
        ),
        "product_b",
    )
    features_c = after(features, keep_b)
    keep_c, send_c = product(
        where, features_c, [bf_lo, bf_hi], (((0, 0, half), (1, 0, half)),), "product_c"
    )
    core_b = shift(after(send_b, keep_c), "core", 1)
    core_c = shift(send_c, "core", 1)
    even, odd = reduce_z(
        where, keep_own, core_own, keep_a, core_a, keep_b, core_b, keep_c, core_c
    )
    summed = small_call(sum_kernel, block, even, shift(odd, "group", 1), name="sum")

    out32 = jax.ShapeDtypeStruct((BLK, BLK), F32)
    state = (to_owner(summed), master, first_moment, second_moment)
    own = small_call(functools.partial(refresh_kernel, scale), block, *state, name="refresh")
    master_out, first_out, second_out = small_call(
        functools.partial(update_kernel, scale), (out32, out32, out32), *state, name="update"
    )
    rollout = gather_rows(where, own, master_out)
    return (master_out, first_out, second_out, rollout, attended)


def solution(mesh):
    fine = Mesh(mesh.devices.reshape(SIZES), AXES)
    rows, cols = ("group", "z", "core"), ("ylo", "x")
    return jax.shard_map(
        local,
        mesh=fine,
        in_specs=(
            P(rows, cols),
            P(rows, cols),
            P(rows, cols),
            P(rows, cols),
            P(rows, cols),
            P(rows, cols),
            P(rows, None, cols),
            P(rows, None, cols),
            P(rows, cols),
            P(rows),
        ),
        out_specs=(
            P(rows, cols),
            P(rows, cols),
            P(rows, cols),
            P(None, cols),
            P(rows, cols),
        ),
        check_vma=False,
    )
```
